1024 devices in a mesh: clip: 16 (over y, core), seq: 16 (over z), help: 4 (over x).
Axes of the slice: x: 4, y: 8, z: 16, core: 2. Of those that a mesh axis runs over, the one named last changes fastest.
Arguments:
- query_states: bfloat16 [131072, 2048], P(('clip', 'seq', 'help')), parts along dimension 0, may hold values from -8 to 8
- key_states: bfloat16 [131072, 2048], P(('clip', 'seq', 'help')), parts along dimension 0, may hold values from -8 to 8
- value_states: bfloat16 [131072, 2048], P(('clip', 'seq', 'help')), parts along dimension 0, may hold values from -6 to 6
- tile_lists: int32 [256, 64, 16], P('clip'), parts along dimension 0, may hold values from 0 to 63, as said below
- tile_counts: int32 [256, 64], P('clip'), parts along dimension 0, may hold values from 1 to 16, as said below
Outputs:
- attended: bfloat16 [131072, 2048], P(('clip', 'seq', 'help')), parts along dimension 0
The draws below stay inside these ranges and needn't reach their ends.
There are 16 independent parts, one for each index of `clip`. The reference program is written for one: setup_inputs(seed, part) draws one part's arguments, and reference() takes and returns one part's arrays. A program takes and returns all parts, laid end to end along the dimension named above; each array names one. Nothing has to cross between parts.
Inputs may be any that keep to these rules, and one draw needn't show every extreme that they name: tile_lists[h, t, :] holds 16 different key tiles, the first of which is t itself; the entries at slots tile_counts[h, t] and beyond are ignored. `tile_counts`: in every head some query tile has count 16.
All inputs are finite; a program needn't handle non-finite values.
Results may differ from the reference program's by a relative error of at most 0.0044.
Values may be sent and summed in bfloat16 or wider, within the bound.
A program may use at most 32 MiB of HBM per device.

```python
import jax
import jax.numpy as jnp
from jax import lax

H = 16
DH = 128
TILE = 128
SEQ_LEN = 8192
QT = 64
SLOTS = 16
D = 2048


def tile_plan(key):
    base = jax.random.fold_in(key, 4242)
    heavy_key, raw_key, place_key, order_key = jax.random.split(base, 4)
    heavy = jax.random.randint(heavy_key, (H, QT), 0, 4) == 0
    ceiling = jnp.where(heavy, SLOTS, max(SLOTS // 4, 1))
    raw_counts = jax.random.randint(raw_key, (H, QT), 0, QT)
    counts = 1 + raw_counts % ceiling
    forced_tile = jax.random.randint(place_key, (H, 1), 0, QT)
    tile_index = jnp.arange(QT, dtype=jnp.int32)[None, :]
    counts = jnp.where(tile_index == forced_tile, SLOTS, counts).astype(jnp.int32)
    ranking = jax.random.randint(order_key, (H, QT, QT), 0, 1 << 20) * QT
    ranking = ranking + jnp.arange(QT, dtype=jnp.int32)[None, None, :]
    own_tile = jnp.arange(QT, dtype=jnp.int32)[:, None] == jnp.arange(QT, dtype=jnp.int32)[None, :]
    ranking = jnp.where(own_tile[None, :, :], -1, ranking)
    lists = jnp.argsort(ranking, axis=-1)[:, :, :SLOTS].astype(jnp.int32)
    return (lists, counts)


def draw_tile_lists(key, part):
    return tile_plan(key)[0]


def draw_tile_counts(key, part):
    return tile_plan(key)[1]


def draw_query_states(key, part):
    own_key = jax.random.fold_in(key, 1)
    states = jax.random.normal(own_key, (SEQ_LEN, D), jnp.float32)
    return jnp.clip(states, -8.0, 8.0).astype(jnp.bfloat16)


def draw_key_states(key, part):
    own_key = jax.random.fold_in(key, 2)
    states = jax.random.normal(own_key, (SEQ_LEN, D), jnp.float32)
    return jnp.clip(states, -8.0, 8.0).astype(jnp.bfloat16)


def level_of(key, shape, pieces, least, top_value):
    loudness, own = 1.0, jax.random.fold_in(key, 6)
    for dim, blocks in pieces:
        steps = jnp.exp(jax.random.uniform(jax.random.fold_in(own, dim), (blocks,), jnp.float32, least / len(pieces), top_value / len(pieces)))
        loudness = loudness * jnp.repeat(steps, shape[dim] // blocks).reshape([-1 if axis == dim else 1 for axis in range(len(shape))])
    return loudness


def normal_values(rng, shape, spread, reach, cuts=(), kind=jnp.bfloat16):
    entries = jax.random.normal(rng, shape, jnp.float32) * spread
    if len(cuts) > 0:
        entries = level_of(rng, shape, cuts, -0.22, 0.18) * entries
    return jnp.clip(entries, min=-reach, max=reach).astype(kind)


def setup_inputs(seed: int = 0, part: int = 0) -> dict:
    key_of = jax.random.split(jax.random.key(seed), 6)
    part_splits = jax.random.split(jax.random.fold_in(key_of[5], part), 6)
    query_states = draw_query_states(jax.random.fold_in(jax.random.fold_in(key_of[5], part), 71), part)
    key_states = draw_key_states(jax.random.fold_in(jax.random.fold_in(key_of[5], part), 71), part)
    value_states = normal_values(part_splits[2], (SEQ_LEN, D), 1.0, 6.0, ((0, 64),))
    tile_lists = draw_tile_lists(jax.random.fold_in(jax.random.fold_in(key_of[5], part), 71), part)
    tile_counts = draw_tile_counts(jax.random.fold_in(jax.random.fold_in(key_of[5], part), 71), part)
    return {"query_states": query_states, "key_states": key_states, "value_states": value_states, "tile_lists": tile_lists, "tile_counts": tile_counts}


big_negative = -1e30


def attend_tiles(query_tiles, key_tiles, value_tiles, tile_lists, tile_counts):
    row_tiles, tile_rows, head_width = query_tiles.shape
    factor = head_width ** -0.5
    query_float = query_tiles.astype(jnp.float32)
    start_state = (jnp.full((row_tiles, tile_rows, 1), big_negative, jnp.float32),
                   jnp.zeros((row_tiles, tile_rows, 1), jnp.float32),
                   jnp.zeros((row_tiles, tile_rows, head_width), jnp.float32))

    def one_slot(slot_index, carried):
        running_max, running_sum, weighted = carried
        chosen = lax.dynamic_index_in_dim(tile_lists, slot_index, axis=1, keepdims=False)
        key_block = jnp.take(key_tiles, chosen, axis=0).astype(jnp.float32)
        value_block = jnp.take(value_tiles, chosen, axis=0).astype(jnp.float32)
        scores = jnp.einsum("qtd,qsd->qts", query_float, key_block) * factor
        new_max = jnp.maximum(running_max, jnp.max(scores, axis=2, keepdims=True))
        shrink = jnp.exp(running_max - new_max)
        tile_weights = jnp.exp(scores - new_max)
        new_sum = running_sum * shrink + jnp.sum(tile_weights, axis=2, keepdims=True)
        rounded = lax.optimization_barrier(tile_weights.astype(jnp.bfloat16)).astype(jnp.float32)
        new_weighted = weighted * shrink + jnp.einsum("qts,qsd->qtd", rounded, value_block)
        live = (slot_index < tile_counts)[:, None, None]
        return (jnp.where(live, new_max, running_max),
                jnp.where(live, new_sum, running_sum),
                jnp.where(live, new_weighted, weighted))

    final_state = lax.fori_loop(0, jnp.max(tile_counts), one_slot, start_state)
    return (final_state[2] / final_state[1]).astype(jnp.bfloat16)


def reference(query_states, key_states, value_states, tile_lists, tile_counts):
    seq_total, model_width = query_states.shape
    tile_total = seq_total // TILE

    def by_head(states):
        return states.reshape(tile_total, TILE, H, DH).transpose(2, 0, 1, 3)

    attended = lax.map(lambda packed: attend_tiles(*packed),
                       (by_head(query_states), by_head(key_states), by_head(value_states), tile_lists, tile_counts))
    return attended.transpose(1, 2, 0, 3).reshape(seq_total, model_width)
```

```python
import functools
import math

import jax
import jax.numpy as jnp
from jax import lax
from jax.experimental import pallas as pl
from jax.experimental.pallas import tpu as pltpu
from jax.sharding import PartitionSpec as P

MESH = pl.DeviceIdType.MESH
TILE = 128
DH = 128
SLOTS = 16


def spread(n, i):
    half = (i + 1) // 2
    return (half * (2 * (i % 2) - 1) + n) % n


def kernel(
    groups, helpers,
    lists_hbm, counts_hbm, q_hbm, k_hbm, v_hbm, out_hbm,
    kv, qs, outs, scores, landed, lists, counts,
    plan_sem, own_sem, send_q, send_kv, send_o, send_x,
    recv_q, recv_kv, recv_o, recv_x, recv_far, write_sem,
):
    z = lax.axis_index("seq")
    x = lax.axis_index("help")
    right = (x + 1) % helpers
    left = (x + helpers - 1) % helpers
    across = (x + 2) % helpers
    mine = z * helpers + x

    plan = [
        pltpu.make_async_copy(lists_hbm.at[z], lists, plan_sem.at[0]),
        pltpu.make_async_copy(counts_hbm, counts, plan_sem.at[1]),
    ]
    for copy in plan:
        copy.start()

    def columns(head):
        return pl.ds(pl.multiple_of(head * DH, DH), DH)

    own = [
        pltpu.make_async_copy(k_hbm.at[:, columns(z)], kv.at[mine, 0], recv_kv.at[z]),
        pltpu.make_async_copy(v_hbm.at[:, columns(z)], kv.at[mine, 1], recv_kv.at[z]),
        pltpu.make_async_copy(q_hbm.at[:, columns(z)], qs.at[z], recv_q.at[z]),
    ]
    for copy in own:
        copy.start()

    barrier = pltpu.get_barrier_semaphore()

    def greet(i, carry):
        pl.semaphore_signal(
            barrier, inc=1, device_id={"seq": (z + i) % groups}, device_id_type=MESH
        )
        return carry

    lax.fori_loop(1, groups, greet, 0)
    for near in (left, right):
        pl.semaphore_signal(barrier, inc=1, device_id={"help": near}, device_id_type=MESH)
    pl.semaphore_wait(barrier, groups + 1)

    def send_keys(i, carry):
        there = (z + spread(groups, i)) % groups
        for which, source in ((0, k_hbm), (1, v_hbm)):
            pltpu.make_async_remote_copy(
                src_ref=source.at[:, columns(there)],
                dst_ref=kv.at[mine, which],
                send_sem=send_kv.at[which],
                recv_sem=recv_kv.at[z],
                device_id={"seq": there},
                device_id_type=MESH,
            ).start()
        return carry

    def send_queries(i, carry):
        there = (z + spread(groups, i)) % groups
        pltpu.make_async_remote_copy(
            src_ref=q_hbm.at[:, columns(there)],
            dst_ref=qs.at[z],
            send_sem=send_q,
            recv_sem=recv_q.at[z],
            device_id={"seq": there},
            device_id_type=MESH,
        ).start()
        return carry

    lax.fori_loop(1, groups, send_keys, 0)
    lax.fori_loop(1, groups, send_queries, 0)

    def tile_copy(tile, way, sem, send, near):
        return pltpu.make_async_remote_copy(
            src_ref=kv.at[tile],
            dst_ref=kv.at[tile],
            send_sem=send_x.at[send],
            recv_sem=sem,
            device_id={"help": near},
            device_id_type=MESH,
        )

    def arrived(ref, sem):
        pltpu.make_async_copy(ref, ref, sem).wait()

    def pass_on(i, carry):
        source = (z + spread(groups, i)) % groups
        tile = source * helpers + x
        arrived(kv.at[tile], recv_kv.at[source])
        tile_copy(tile, 0, recv_x.at[0, source], 0, right).start()
        tile_copy(tile, 1, recv_x.at[1, source], 1, left).start()
        return carry

    def pass_far(i, carry):
        even = (z + spread(groups, i)) % groups
        odd = (z + spread(groups, i + 1)) % groups
        from_left = even * helpers + left
        from_right = odd * helpers + right
        arrived(kv.at[from_left], recv_x.at[0, even])
        tile_copy(from_left, 0, recv_far.at[even], 2, right).start()
        arrived(kv.at[from_right], recv_x.at[1, odd])
        tile_copy(from_right, 1, recv_far.at[odd], 2, left).start()
        return carry

    lax.fori_loop(0, groups, pass_on, 0)
    lax.fori_loop(0, groups // 2, lambda i, c: pass_far(2 * i, c), 0)

    def rest(i, carry):
        even = (z + spread(groups, 2 * i)) % groups
        odd = (z + spread(groups, 2 * i + 1)) % groups
        arrived(kv.at[odd * helpers + left], recv_x.at[0, odd])
        arrived(kv.at[even * helpers + right], recv_x.at[1, even])
        arrived(kv.at[even * helpers + across], recv_far.at[even])
        arrived(kv.at[odd * helpers + across], recv_far.at[odd])
        return carry

    lax.fori_loop(0, groups // 2, rest, 0)
    for copy in plan:
        copy.wait()

    scale = DH**-0.5 * math.log2(math.e)

    def attend(i, carry):
        source = (z + spread(groups, i)) % groups
        tile = source * helpers + x
        arrived(qs.at[source], recv_q.at[source])
        query = qs[source]
        count = counts[z, tile]
        first = lists[tile, 0]
        chosen = [first] + [
            jnp.where(j < count, lists[tile, j], first) for j in range(1, SLOTS)
        ]
        most = None
        for j in range(0, SLOTS, 2):
            keys = jnp.concatenate((kv[chosen[j], 0], kv[chosen[j + 1], 0]), axis=0)
            part = lax.dot_general(
                query, keys, (((1,), (1,)), ((), ())), preferred_element_type=jnp.float32
            )
            scores[j // 2] = part
            most = part if most is None else jnp.maximum(most, part)
        top = jnp.max(most, axis=1, keepdims=True) * scale
        total = jnp.zeros((TILE, DH), jnp.float32)
        mixed = jnp.zeros((TILE, DH), jnp.float32)
        for j in range(0, SLOTS, 2):
            weights = []
            for k in (j, j + 1):
                shift = top + jnp.where(k < count, 0.0, 1e30).astype(jnp.float32)
                part = scores[j // 2, :, (k - j) * TILE : (k - j + 1) * TILE]
                weight = jnp.exp2(part * scale - shift)
                total += weight
                weights.append(weight.astype(jnp.bfloat16))
            values = jnp.concatenate((kv[chosen[j], 1], kv[chosen[j + 1], 1]), axis=0)
            mixed += lax.dot_general(
                jnp.concatenate(weights, axis=1),
                values,
                (((1,), (0,)), ((), ())),
                preferred_element_type=jnp.float32,
            )
        outs[source] = (mixed / jnp.sum(total, axis=1, keepdims=True)).astype(jnp.bfloat16)

        @pl.when(i == 0)
        def _():
            pltpu.make_async_copy(outs.at[z], landed.at[:, columns(z)], recv_o.at[z]).start()

        @pl.when(i > 0)
        def _():
            pltpu.make_async_remote_copy(
                src_ref=outs.at[source],
                dst_ref=landed.at[:, columns(z)],
                send_sem=send_o,
                recv_sem=recv_o.at[z],
                device_id={"seq": source},
                device_id_type=MESH,
            ).start()

        return carry

    lax.fori_loop(0, groups, attend, 0)

    away = groups - 1
    for which in (0, 1):
        arrived(kv.at[pl.ds(0, away), which], send_kv.at[which])
    arrived(qs.at[pl.ds(0, away)], send_q)
    for which in (0, 1):
        arrived(kv.at[pl.ds(0, groups)], send_x.at[which])
    arrived(kv.at[pl.ds(0, groups)], send_x.at[2])

    def take(i, carry):
        head = (z + spread(groups, i)) % groups
        arrived(landed.at[:, columns(head)], recv_o.at[head])
        return carry

    lax.fori_loop(0, groups, take, 0)
    arrived(outs.at[pl.ds(0, away)], send_o)
    write = pltpu.make_async_copy(landed, out_hbm, write_sem)
    write.start()
    write.wait()


def solution(mesh):
    groups, helpers = mesh.shape["seq"], mesh.shape["help"]
    tiles = groups * helpers
    dma = pltpu.SemaphoreType.DMA

    def shards(query_states, key_states, value_states, tile_lists, tile_counts):
        heads = tile_lists.shape[0]
        return pl.pallas_call(
            functools.partial(kernel, groups, helpers),
            out_shape=jax.ShapeDtypeStruct(query_states.shape, jnp.bfloat16),
            in_specs=[pl.BlockSpec(memory_space=pl.ANY)] * 5,
            out_specs=pl.BlockSpec(memory_space=pl.ANY),
            scratch_shapes=[
                pltpu.VMEM((tiles, 2, TILE, DH), jnp.bfloat16),
                pltpu.VMEM((groups, TILE, DH), jnp.bfloat16),
                pltpu.VMEM((groups, TILE, DH), jnp.bfloat16),
                pltpu.VMEM((SLOTS // 2, TILE, 2 * TILE), jnp.float32),
                pltpu.VMEM((TILE, groups * DH), jnp.bfloat16),
                pltpu.SMEM((tiles, SLOTS), jnp.int32),
                pltpu.SMEM((heads, tiles), jnp.int32),
                dma((2,)),
                dma((1,)),
                dma,
                dma((2,)),
                dma,
                dma((3,)),
                dma((groups,)),
                dma((groups,)),
                dma((groups,)),
                dma((2, groups)),
                dma((groups,)),
                dma,
            ],
            compiler_params=pltpu.CompilerParams(
                collective_id=0, has_side_effects=True, vmem_limit_bytes=24 * 2**20
            ),
            cost_estimate=pl.CostEstimate(
                flops=4 * groups * SLOTS * TILE**3,
                bytes_accessed=4 * TILE * groups * DH * 2,
                transcendentals=groups * SLOTS * TILE**2,
            ),
        )(tile_lists, tile_counts, query_states, key_states, value_states)

    rows = P(("clip", "seq", "help"), None)
    return jax.shard_map(
        shards,
        mesh=mesh,
        in_specs=(rows, rows, rows, P("clip", None, None), P("clip", None)),
        out_specs=rows,
        check_vma=False,
    )
```

```python
import functools
import math

import jax
import jax.numpy as jnp
from jax import lax
from jax.experimental import pallas as pl
from jax.experimental.pallas import tpu as pltpu
from jax.sharding import PartitionSpec as P

MESH = pl.DeviceIdType.MESH
TILE = 128
DH = 128
SLOTS = 16


def spread(n, i):
    half = (i + 1) // 2
    return (half * (2 * (i % 2) - 1) + n) % n


def kernel(
    groups, helpers,
    lists_hbm, counts_hbm, q_hbm, k_hbm, v_hbm, out_ref,
    kv, qs, outs, scores, lists, counts,
    plan_sem, up, down, send_q, send_kv, send_o, send_x,
    recv_q, recv_kv, recv_o, recv_x, recv_far,
):
    z = lax.axis_index("seq")
    x = lax.axis_index("help")
    right = (x + 1) % helpers
    left = (x + helpers - 1) % helpers
    across = (x + 2) % helpers
    above = (z + 1) % groups
    below = (z + groups - 1) % groups
    half = groups // 2
    mine = z * helpers + x

    barrier = pltpu.get_barrier_semaphore()
    for near in (above, below):
        pl.semaphore_signal(barrier, inc=1, device_id={"seq": near}, device_id_type=MESH)
    for near in (left, right):
        pl.semaphore_signal(barrier, inc=1, device_id={"help": near}, device_id_type=MESH)

    plan = [
        pltpu.make_async_copy(lists_hbm.at[z], lists, plan_sem.at[0]),
        pltpu.make_async_copy(counts_hbm, counts, plan_sem.at[1]),
    ]
    for copy in plan:
        copy.start()

    def columns(head):
        return pl.ds(pl.multiple_of(head * DH, DH), DH)

    own = [
        pltpu.make_async_copy(k_hbm.at[:, columns(z)], kv.at[mine, 0], recv_kv.at[z]),
        pltpu.make_async_copy(v_hbm.at[:, columns(z)], kv.at[mine, 1], recv_kv.at[z]),
        pltpu.make_async_copy(q_hbm.at[:, columns(z)], qs.at[z], recv_q.at[z]),
    ]
    for copy in own:
        copy.start()

    def send_keys(there):
        for which, source in ((0, k_hbm), (1, v_hbm)):
            pltpu.make_async_remote_copy(
                src_ref=source.at[:, columns(there)],
                dst_ref=kv.at[mine, which],
                send_sem=send_kv.at[which],
                recv_sem=recv_kv.at[z],
                device_id={"seq": there},
                device_id_type=MESH,
            ).start()

    def tell(distance):
        pl.semaphore_signal(
            up.at[distance + 1], inc=1, device_id={"seq": above}, device_id_type=MESH
        )
        pl.semaphore_signal(
            down.at[distance + 1], inc=1, device_id={"seq": below}, device_id_type=MESH
        )

    pl.semaphore_wait(barrier, 4)
    tell(1)
    send_keys(above)
    send_keys(below)

    def wave(distance, carry):
        pl.semaphore_wait(up.at[distance], 1)
        pl.semaphore_wait(down.at[distance], 1)
        tell(distance)
        send_keys((z + distance) % groups)
        send_keys((z + groups - distance) % groups)
        return carry

    lax.fori_loop(2, half, wave, 0)
    pl.semaphore_wait(up.at[half], 1)
    pl.semaphore_wait(down.at[half], 1)
    send_keys((z + half) % groups)

    def send_queries(i, carry):
        there = (z + spread(groups, groups - 1 - i)) % groups
        pltpu.make_async_remote_copy(
            src_ref=q_hbm.at[:, columns(there)],
            dst_ref=qs.at[z],
            send_sem=send_q,
            recv_sem=recv_q.at[z],
            device_id={"seq": there},
            device_id_type=MESH,
        ).start()
        return carry

    lax.fori_loop(0, groups - 1, send_queries, 0)

    def tile_copy(tile, sem, send, near):
        return pltpu.make_async_remote_copy(
            src_ref=kv.at[tile],
            dst_ref=kv.at[tile],
            send_sem=send_x.at[send],
            recv_sem=sem,
            device_id={"help": near},
            device_id_type=MESH,
        )

    def arrived(ref, sem):
        pltpu.make_async_copy(ref, ref, sem).wait()

    def pass_on(i, carry):
        source = (z + spread(groups, i)) % groups
        tile = source * helpers + x
        arrived(kv.at[tile], recv_kv.at[source])
        tile_copy(tile, recv_x.at[0, source], 0, right).start()
        tile_copy(tile, recv_x.at[1, source], 1, left).start()
        return carry

    def pass_far(i):
        even = (z + spread(groups, i)) % groups
        odd = (z + spread(groups, i + 1)) % groups
        from_left = even * helpers + left
        from_right = odd * helpers + right
        arrived(kv.at[from_left], recv_x.at[0, even])
        tile_copy(from_left, recv_far.at[even], 2, right).start()
        arrived(kv.at[from_right], recv_x.at[1, odd])
        tile_copy(from_right, recv_far.at[odd], 2, left).start()

    def pass_both(i, carry):
        pass_on(2 * i, 0)
        pass_on(2 * i + 1, 0)
        pass_far(2 * i - 2)
        return carry

    pass_on(0, 0)
    pass_on(1, 0)
    lax.fori_loop(1, half, pass_both, 0)
    pass_far(groups - 2)

    def rest(i, carry):
        even = (z + spread(groups, 2 * i)) % groups
        odd = (z + spread(groups, 2 * i + 1)) % groups
        arrived(kv.at[odd * helpers + left], recv_x.at[0, odd])
        arrived(kv.at[even * helpers + right], recv_x.at[1, even])
        arrived(kv.at[even * helpers + across], recv_far.at[even])
        arrived(kv.at[odd * helpers + across], recv_far.at[odd])
        return carry

    lax.fori_loop(0, half, rest, 0)
    for copy in plan:
        copy.wait()

    scale = DH**-0.5 * math.log2(math.e)

    def attend(i, carry):
        source = (z + spread(groups, groups - 1 - i)) % groups
        tile = source * helpers + x
        arrived(qs.at[source], recv_q.at[source])
        query = qs[source]
        count = counts[z, tile]
        first = lists[0, tile]
        chosen = [first] + [
            jnp.where(j < count, lists[j, tile], first) for j in range(1, SLOTS)
        ]
        most = None
        for j in range(0, SLOTS, 2):
            keys = jnp.concatenate((kv[chosen[j], 0], kv[chosen[j + 1], 0]), axis=0)
            part = lax.dot_general(
                query, keys, (((1,), (1,)), ((), ())), preferred_element_type=jnp.float32
            )
            scores[j // 2] = part
            most = part if most is None else jnp.maximum(most, part)
        top = jnp.max(most, axis=1, keepdims=True) * scale
        total = jnp.zeros((TILE, DH), jnp.float32)
        mixed = jnp.zeros((TILE, DH), jnp.float32)
        for j in range(0, SLOTS, 2):
            weights = []
            for k in (j, j + 1):
                shift = top + jnp.where(k < count, 0.0, 1e30).astype(jnp.float32)
                part = scores[j // 2, :, (k - j) * TILE : (k - j + 1) * TILE]
                weight = jnp.exp2(part * scale - shift)
                total += weight
                weights.append(weight.astype(jnp.bfloat16))
            values = jnp.concatenate((kv[chosen[j], 1], kv[chosen[j + 1], 1]), axis=0)
            mixed += lax.dot_general(
                jnp.concatenate(weights, axis=1),
                values,
                (((1,), (0,)), ((), ())),
                preferred_element_type=jnp.float32,
            )
        outs[source] = (mixed / jnp.sum(total, axis=1, keepdims=True)).astype(jnp.bfloat16)

        @pl.when(i == groups - 1)
        def _():
            pltpu.make_async_copy(outs.at[z], out_ref.at[:, columns(z)], recv_o.at[z]).start()

        @pl.when(i < groups - 1)
        def _():
            pltpu.make_async_remote_copy(
                src_ref=outs.at[source],
                dst_ref=out_ref.at[:, columns(z)],
                send_sem=send_o,
                recv_sem=recv_o.at[z],
                device_id={"seq": source},
                device_id_type=MESH,
            ).start()

        return carry

    lax.fori_loop(0, groups, attend, 0)

    away = groups - 1
    for which in (0, 1):
        arrived(kv.at[pl.ds(0, away), which], send_kv.at[which])
    arrived(qs.at[pl.ds(0, away)], send_q)
    for which in (0, 1, 2):
        arrived(kv.at[pl.ds(0, groups)], send_x.at[which])

    def take(i, carry):
        arrived(out_ref.at[:, columns(i)], recv_o.at[i])
        return carry

    lax.fori_loop(0, groups, take, 0)
    arrived(outs.at[pl.ds(0, away)], send_o)


def solution(mesh):
    groups, helpers = mesh.shape["seq"], mesh.shape["help"]
    tiles = groups * helpers
    dma = pltpu.SemaphoreType.DMA

    def shards(query_states, key_states, value_states, tile_lists, tile_counts):
        heads = tile_lists.shape[0]
        return pl.pallas_call(
            functools.partial(kernel, groups, helpers),
            out_shape=jax.ShapeDtypeStruct(query_states.shape, jnp.bfloat16),
            in_specs=[pl.BlockSpec(memory_space=pl.ANY)] * 5,
            out_specs=pl.BlockSpec(memory_space=pl.ANY),
            scratch_shapes=[
                pltpu.VMEM((tiles, 2, TILE, DH), jnp.bfloat16),
                pltpu.VMEM((groups, TILE, DH), jnp.bfloat16),
                pltpu.VMEM((groups, TILE, DH), jnp.bfloat16),
                pltpu.VMEM((SLOTS // 2, TILE, 2 * TILE), jnp.float32),
                pltpu.SMEM((SLOTS, tiles), jnp.int32),
                pltpu.SMEM((heads, tiles), jnp.int32),
                dma((2,)),
                pltpu.SemaphoreType.REGULAR((groups // 2 + 1,)),
                pltpu.SemaphoreType.REGULAR((groups // 2 + 1,)),
                dma,
                dma((2,)),
                dma,
                dma((3,)),
                dma((groups,)),
                dma((groups,)),
                dma((groups,)),
                dma((2, groups)),
                dma((groups,)),
            ],
            compiler_params=pltpu.CompilerParams(
                collective_id=0, has_side_effects=True, vmem_limit_bytes=60 * 2**20
            ),
            cost_estimate=pl.CostEstimate(
                flops=4 * groups * SLOTS * TILE**3,
                bytes_accessed=4 * TILE * groups * DH * 2,
                transcendentals=groups * SLOTS * TILE**2,
            ),
        )(jnp.swapaxes(tile_lists, 1, 2), tile_counts, query_states, key_states, value_states)

    rows = P(("clip", "seq", "help"), None)
    return jax.shard_map(
        shards,
        mesh=mesh,
        in_specs=(rows, rows, rows, P("clip", None, None), P("clip", None)),
        out_specs=rows,
        check_vma=False,
    )
```

```python
import functools
import math

import jax
import jax.numpy as jnp
from jax import lax
from jax.experimental import pallas as pl
from jax.experimental.pallas import tpu as pltpu
from jax.sharding import PartitionSpec as P

MESH = pl.DeviceIdType.MESH
TILE = 128
DH = 128
SLOTS = 16


def spread(n, i):
    half = (i + 1) // 2
    return (half * (2 * (i % 2) - 1) + n) % n


def kernel(
    groups, helpers,
    lists_hbm, counts_hbm, q_hbm, k_hbm, v_hbm, out_ref,
    kv, qs, outs, scores, lists, counts,
    plan_sem, up, down, send_q, send_kv, send_o, send_x,
    recv_q, recv_kv, recv_o, recv_x, recv_far,
):
    z = lax.axis_index("seq")
    x = lax.axis_index("help")
    right = (x + 1) % helpers
    left = (x + helpers - 1) % helpers
    across = (x + 2) % helpers
    above = (z + 1) % groups
    below = (z + groups - 1) % groups
    half = groups // 2
    mine = z * helpers + x

    barrier = pltpu.get_barrier_semaphore()
    for near in (above, below):
        pl.semaphore_signal(barrier, inc=1, device_id={"seq": near}, device_id_type=MESH)
    for near in (left, right):
        pl.semaphore_signal(barrier, inc=1, device_id={"help": near}, device_id_type=MESH)

    plan = [
        pltpu.make_async_copy(lists_hbm.at[z], lists, plan_sem.at[0]),
        pltpu.make_async_copy(counts_hbm, counts, plan_sem.at[1]),
    ]
    for copy in plan:
        copy.start()

    def columns(head):
        return pl.ds(pl.multiple_of(head * DH, DH), DH)

    own = [
        pltpu.make_async_copy(k_hbm.at[:, columns(z)], kv.at[mine, 0], recv_kv.at[z]),
        pltpu.make_async_copy(v_hbm.at[:, columns(z)], kv.at[mine, 1], recv_kv.at[z]),
        pltpu.make_async_copy(q_hbm.at[:, columns(z)], qs.at[z], recv_q.at[z]),
    ]
    for copy in own:
        copy.start()

    def send_keys(there):
        for which, source in ((0, k_hbm), (1, v_hbm)):
            pltpu.make_async_remote_copy(
                src_ref=source.at[:, columns(there)],
                dst_ref=kv.at[mine, which],
                send_sem=send_kv.at[which],
                recv_sem=recv_kv.at[z],
                device_id={"seq": there},
                device_id_type=MESH,
            ).start()

    def tell(distance):
        pl.semaphore_signal(
            up.at[distance + 1], inc=1, device_id={"seq": above}, device_id_type=MESH
        )
        pl.semaphore_signal(
            down.at[distance + 1], inc=1, device_id={"seq": below}, device_id_type=MESH
        )

    pl.semaphore_wait(barrier, 4)
    tell(1)
    send_keys(above)
    send_keys(below)

    def wave(distance, carry):
        pl.semaphore_wait(up.at[distance], 1)
        pl.semaphore_wait(down.at[distance], 1)
        tell(distance)
        send_keys((z + distance) % groups)
        send_keys((z + groups - distance) % groups)
        return carry

    lax.fori_loop(2, half, wave, 0)
    pl.semaphore_wait(up.at[half], 1)
    pl.semaphore_wait(down.at[half], 1)
    send_keys((z + half) % groups)

    def send_queries(i, carry):
        there = (z + spread(groups, i + 1)) % groups
        pltpu.make_async_remote_copy(
            src_ref=q_hbm.at[:, columns(there)],
            dst_ref=qs.at[z],
            send_sem=send_q,
            recv_sem=recv_q.at[z],
            device_id={"seq": there},
            device_id_type=MESH,
        ).start()
        return carry

    lax.fori_loop(0, groups - 1, send_queries, 0)

    def tile_copy(tile, sem, send, near):
        return pltpu.make_async_remote_copy(
            src_ref=kv.at[tile],
            dst_ref=kv.at[tile],
            send_sem=send_x.at[send],
            recv_sem=sem,
            device_id={"help": near},
            device_id_type=MESH,
        )

    def arrived(ref, sem):
        pltpu.make_async_copy(ref, ref, sem).wait()

    def pass_on(i, carry):
        source = (z + spread(groups, i)) % groups
        tile = source * helpers + x
        arrived(kv.at[tile], recv_kv.at[source])
        tile_copy(tile, recv_x.at[0, source], 0, right).start()
        tile_copy(tile, recv_x.at[1, source], 1, left).start()
        return carry

    def pass_far(i):
        even = (z + spread(groups, i)) % groups
        odd = (z + spread(groups, i + 1)) % groups
        from_left = even * helpers + left
        from_right = odd * helpers + right
        arrived(kv.at[from_left], recv_x.at[0, even])
        tile_copy(from_left, recv_far.at[even], 2, right).start()
        arrived(kv.at[from_right], recv_x.at[1, odd])
        tile_copy(from_right, recv_far.at[odd], 2, left).start()

    def pass_both(i, carry):
        pass_on(2 * i, 0)
        pass_on(2 * i + 1, 0)
        pass_far(2 * i - 2)
        return carry

    pass_on(0, 0)
    pass_on(1, 0)
    lax.fori_loop(1, half, pass_both, 0)
    pass_far(groups - 2)

    def rest(i, carry):
        even = (z + spread(groups, 2 * i)) % groups
        odd = (z + spread(groups, 2 * i + 1)) % groups
        arrived(kv.at[odd * helpers + left], recv_x.at[0, odd])
        arrived(kv.at[even * helpers + right], recv_x.at[1, even])
        arrived(kv.at[even * helpers + across], recv_far.at[even])
        arrived(kv.at[odd * helpers + across], recv_far.at[odd])
        return carry

    lax.fori_loop(0, half, rest, 0)
    for copy in plan:
        copy.wait()

    scale = DH**-0.5 * math.log2(math.e)

    def attend(i, carry):
        source = (i // 4) * 4 + (z + i) % 4
        tile = source * helpers + x
        arrived(qs.at[source], recv_q.at[source])
        query = qs[source]
        count = counts[z, tile]
        first = lists[0, tile]
        chosen = [first] + [
            jnp.where(j < count, lists[j, tile], first) for j in range(1, SLOTS)
        ]
        most = None
        for j in range(0, SLOTS, 2):
            keys = jnp.concatenate((kv[chosen[j], 0], kv[chosen[j + 1], 0]), axis=0)
            part = lax.dot_general(
                query, keys, (((1,), (1,)), ((), ())), preferred_element_type=jnp.float32
            )
            scores[j // 2] = part
            most = part if most is None else jnp.maximum(most, part)
        top = jnp.max(most, axis=1, keepdims=True) * scale
        total = jnp.zeros((TILE, DH), jnp.float32)
        mixed = jnp.zeros((TILE, DH), jnp.float32)
        for j in range(0, SLOTS, 2):
            weights = []
            for k in (j, j + 1):
                shift = top + jnp.where(k < count, 0.0, 1e30).astype(jnp.float32)
                part = scores[j // 2, :, (k - j) * TILE : (k - j + 1) * TILE]
                weight = jnp.exp2(part * scale - shift)
                total += weight
                weights.append(weight.astype(jnp.bfloat16))
            values = jnp.concatenate((kv[chosen[j], 1], kv[chosen[j + 1], 1]), axis=0)
            mixed += lax.dot_general(
                jnp.concatenate(weights, axis=1),
                values,
                (((1,), (0,)), ((), ())),
                preferred_element_type=jnp.float32,
            )
        outs[source] = (mixed / jnp.sum(total, axis=1, keepdims=True)).astype(jnp.bfloat16)

        @pl.when(source == z)
        def _():
            pltpu.make_async_copy(outs.at[z], out_ref.at[:, columns(z)], recv_o.at[z]).start()

        @pl.when(source != z)
        def _():
            pltpu.make_async_remote_copy(
                src_ref=outs.at[source],
                dst_ref=out_ref.at[:, columns(z)],
                send_sem=send_o,
                recv_sem=recv_o.at[z],
                device_id={"seq": source},
                device_id_type=MESH,
            ).start()

        return carry

    lax.fori_loop(0, groups, attend, 0)

    away = groups - 1
    for which in (0, 1):
        arrived(kv.at[pl.ds(0, away), which], send_kv.at[which])
    arrived(qs.at[pl.ds(0, away)], send_q)
    for which in (0, 1, 2):
        arrived(kv.at[pl.ds(0, groups)], send_x.at[which])

    def take(i, carry):
        arrived(out_ref.at[:, columns(i)], recv_o.at[i])
        return carry

    lax.fori_loop(0, groups, take, 0)
    arrived(outs.at[pl.ds(0, away)], send_o)


def solution(mesh):
    groups, helpers = mesh.shape["seq"], mesh.shape["help"]
    tiles = groups * helpers
    dma = pltpu.SemaphoreType.DMA

    def shards(query_states, key_states, value_states, tile_lists, tile_counts):
        heads = tile_lists.shape[0]
        return pl.pallas_call(
            functools.partial(kernel, groups, helpers),
            out_shape=pltpu.VMEM(query_states.shape, jnp.bfloat16),
            in_specs=[pl.BlockSpec(memory_space=pl.ANY)] * 5,
            out_specs=pl.BlockSpec(memory_space=pl.ANY),
            scratch_shapes=[
                pltpu.VMEM((tiles, 2, TILE, DH), jnp.bfloat16),
                pltpu.VMEM((groups, TILE, DH), jnp.bfloat16),
                pltpu.VMEM((groups, TILE, DH), jnp.bfloat16),
                pltpu.VMEM((SLOTS // 2, TILE, 2 * TILE), jnp.float32),
                pltpu.SMEM((SLOTS, tiles), jnp.int32),
                pltpu.SMEM((heads, tiles), jnp.int32),
                dma((2,)),
                pltpu.SemaphoreType.REGULAR((groups // 2 + 1,)),
                pltpu.SemaphoreType.REGULAR((groups // 2 + 1,)),
                dma,
                dma((2,)),
                dma,
                dma((3,)),
                dma((groups,)),
                dma((groups,)),
                dma((groups,)),
                dma((2, groups)),
                dma((groups,)),
            ],
            compiler_params=pltpu.CompilerParams(
                collective_id=0, has_side_effects=True, vmem_limit_bytes=62 * 2**20
            ),
            cost_estimate=pl.CostEstimate(
                flops=4 * groups * SLOTS * TILE**3,
                bytes_accessed=4 * TILE * groups * DH * 2,
                transcendentals=groups * SLOTS * TILE**2,
            ),
        )(jnp.swapaxes(tile_lists, 1, 2), tile_counts, query_states, key_states, value_states)

    rows = P(("clip", "seq", "help"), None)
    return jax.shard_map(
        shards,
        mesh=mesh,
        in_specs=(rows, rows, rows, P("clip", None, None), P("clip", None)),
        out_specs=rows,
        check_vma=False,
    )
```

```python
import functools
import math

import jax
import jax.numpy as jnp
from jax import lax
from jax.experimental import pallas as pl
from jax.experimental.pallas import tpu as pltpu
from jax.sharding import PartitionSpec as P

MESH = pl.DeviceIdType.MESH
TILE = 128
DH = 128
SLOTS = 16


def spread(n, i):
    half = (i + 1) // 2
    return (half * (2 * (i % 2) - 1) + n) % n


def kernel(
    groups, helpers,
    lists_hbm, counts_hbm, q_hbm, k_hbm, v_hbm, out_ref,
    kv, qs, outs, scores, lists, counts,
    plan_sem, up, down, send_q, send_kv, send_o, send_x,
    recv_q, recv_kv, recv_o, recv_x, recv_far,
):
    z = lax.axis_index("seq")
    x = lax.axis_index("help")
    right = (x + 1) % helpers
    left = (x + helpers - 1) % helpers
    across = (x + 2) % helpers
    above = (z + 1) % groups
    below = (z + groups - 1) % groups
    half = groups // 2
    mine = z * helpers + x

    barrier = pltpu.get_barrier_semaphore()
    for near in (above, below):
        pl.semaphore_signal(barrier, inc=1, device_id={"seq": near}, device_id_type=MESH)
    for near in (left, right):
        pl.semaphore_signal(barrier, inc=1, device_id={"help": near}, device_id_type=MESH)

    plan = [
        pltpu.make_async_copy(lists_hbm.at[z], lists, plan_sem.at[0]),
        pltpu.make_async_copy(counts_hbm, counts, plan_sem.at[1]),
    ]
    for copy in plan:
        copy.start()

    def columns(head):
        return pl.ds(pl.multiple_of(head * DH, DH), DH)

    own = [
        pltpu.make_async_copy(k_hbm.at[:, columns(z)], kv.at[mine, 0], recv_kv.at[z]),
        pltpu.make_async_copy(v_hbm.at[:, columns(z)], kv.at[mine, 1], recv_kv.at[z]),
        pltpu.make_async_copy(q_hbm.at[:, columns(z)], qs.at[z], recv_q.at[z]),
    ]
    for copy in own:
        copy.start()

    def send_keys(there):
        for which, source in ((0, k_hbm), (1, v_hbm)):
            pltpu.make_async_remote_copy(
                src_ref=source.at[:, columns(there)],
                dst_ref=kv.at[mine, which],
                send_sem=send_kv.at[which],
                recv_sem=recv_kv.at[z],
                device_id={"seq": there},
                device_id_type=MESH,
            ).start()

    def tell(distance):
        pl.semaphore_signal(
            up.at[distance + 1], inc=1, device_id={"seq": above}, device_id_type=MESH
        )
        pl.semaphore_signal(
            down.at[distance + 1], inc=1, device_id={"seq": below}, device_id_type=MESH
        )

    pl.semaphore_wait(barrier, 4)
    tell(1)
    send_keys(above)
    send_keys(below)

    def wave(distance, carry):
        pl.semaphore_wait(up.at[distance], 1)
        pl.semaphore_wait(down.at[distance], 1)
        tell(distance)
        send_keys((z + distance) % groups)
        send_keys((z + groups - distance) % groups)
        return carry

    lax.fori_loop(2, half, wave, 0)
    pl.semaphore_wait(up.at[half], 1)
    pl.semaphore_wait(down.at[half], 1)
    send_keys((z + half) % groups)

    def turn(i):
        return (i // 4) * 4 + (z + i) % 4

    def send_queries(i, carry):
        there = turn(i)

        @pl.when(there != z)
        def _():
            pltpu.make_async_remote_copy(
                src_ref=q_hbm.at[:, columns(there)],
                dst_ref=qs.at[z],
                send_sem=send_q,
                recv_sem=recv_q.at[z],
                device_id={"seq": there},
                device_id_type=MESH,
            ).start()

        return carry

    lax.fori_loop(0, groups, send_queries, 0)

    def tile_copy(tile, sem, send, near):
        return pltpu.make_async_remote_copy(
            src_ref=kv.at[tile],
            dst_ref=kv.at[tile],
            send_sem=send_x.at[send],
            recv_sem=sem,
            device_id={"help": near},
            device_id_type=MESH,
        )

    def arrived(ref, sem):
        pltpu.make_async_copy(ref, ref, sem).wait()

    def pass_on(i, carry):
        source = (z + spread(groups, i)) % groups
        tile = source * helpers + x
        arrived(kv.at[tile], recv_kv.at[source])
        tile_copy(tile, recv_x.at[0, source], 0, right).start()
        tile_copy(tile, recv_x.at[1, source], 1, left).start()
        return carry

    def pass_far(i):
        even = (z + spread(groups, i)) % groups
        odd = (z + spread(groups, i + 1)) % groups
        from_left = even * helpers + left
        from_right = odd * helpers + right
        arrived(kv.at[from_left], recv_x.at[0, even])
        tile_copy(from_left, recv_far.at[even], 2, right).start()
        arrived(kv.at[from_right], recv_x.at[1, odd])
        tile_copy(from_right, recv_far.at[odd], 2, left).start()

    def pass_both(i, carry):
        pass_on(2 * i, 0)
        pass_on(2 * i + 1, 0)
        pass_far(2 * i - 2)
        return carry

    pass_on(0, 0)
    pass_on(1, 0)
    lax.fori_loop(1, half, pass_both, 0)
    pass_far(groups - 2)

    def rest(i, carry):
        even = (z + spread(groups, 2 * i)) % groups
        odd = (z + spread(groups, 2 * i + 1)) % groups
        arrived(kv.at[odd * helpers + left], recv_x.at[0, odd])
        arrived(kv.at[even * helpers + right], recv_x.at[1, even])
        arrived(kv.at[even * helpers + across], recv_far.at[even])
        arrived(kv.at[odd * helpers + across], recv_far.at[odd])
        return carry

    lax.fori_loop(0, half, rest, 0)
    for copy in plan:
        copy.wait()

    scale = DH**-0.5 * math.log2(math.e)

    def attend(i, carry):
        source = turn(i)
        tile = source * helpers + x
        arrived(qs.at[source], recv_q.at[source])
        query = qs[source]
        count = counts[z, tile]
        first = lists[0, tile]
        chosen = [first] + [
            jnp.where(j < count, lists[j, tile], first) for j in range(1, SLOTS)
        ]
        most = None
        for j in range(0, SLOTS, 2):
            keys = jnp.concatenate((kv[chosen[j], 0], kv[chosen[j + 1], 0]), axis=0)
            part = lax.dot_general(
                query, keys, (((1,), (1,)), ((), ())), preferred_element_type=jnp.float32
            )
            scores[j // 2] = part
            most = part if most is None else jnp.maximum(most, part)
        top = jnp.max(most, axis=1, keepdims=True) * scale
        total = jnp.zeros((TILE, DH), jnp.float32)
        mixed = jnp.zeros((TILE, DH), jnp.float32)
        for j in range(0, SLOTS, 2):
            weights = []
            for k in (j, j + 1):
                shift = top + jnp.where(k < count, 0.0, 1e30).astype(jnp.float32)
                part = scores[j // 2, :, (k - j) * TILE : (k - j + 1) * TILE]
                weight = jnp.exp2(part * scale - shift)
                total += weight
                weights.append(weight.astype(jnp.bfloat16))
            values = jnp.concatenate((kv[chosen[j], 1], kv[chosen[j + 1], 1]), axis=0)
            mixed += lax.dot_general(
                jnp.concatenate(weights, axis=1),
                values,
                (((1,), (0,)), ((), ())),
                preferred_element_type=jnp.float32,
            )
        outs[source] = (mixed / jnp.sum(total, axis=1, keepdims=True)).astype(jnp.bfloat16)

        @pl.when(source == z)
        def _():
            pltpu.make_async_copy(outs.at[z], out_ref.at[:, columns(z)], recv_o.at[z]).start()

        @pl.when(source != z)
        def _():
            pltpu.make_async_remote_copy(
                src_ref=outs.at[source],
                dst_ref=out_ref.at[:, columns(z)],
                send_sem=send_o,
                recv_sem=recv_o.at[z],
                device_id={"seq": source},
                device_id_type=MESH,
            ).start()

        return carry

    lax.fori_loop(0, groups, attend, 0)

    away = groups - 1
    for which in (0, 1):
        arrived(kv.at[pl.ds(0, away), which], send_kv.at[which])
    arrived(qs.at[pl.ds(0, away)], send_q)
    for which in (0, 1, 2):
        arrived(kv.at[pl.ds(0, groups)], send_x.at[which])

    def take(i, carry):
        arrived(out_ref.at[:, columns(i)], recv_o.at[i])
        return carry

    lax.fori_loop(0, groups, take, 0)
    arrived(outs.at[pl.ds(0, away)], send_o)


def solution(mesh):
    groups, helpers = mesh.shape["seq"], mesh.shape["help"]
    tiles = groups * helpers
    dma = pltpu.SemaphoreType.DMA

    def shards(query_states, key_states, value_states, tile_lists, tile_counts):
        heads = tile_lists.shape[0]
        return pl.pallas_call(
            functools.partial(kernel, groups, helpers),
            out_shape=pltpu.VMEM(query_states.shape, jnp.bfloat16),
            in_specs=[pl.BlockSpec(memory_space=pl.ANY)] * 5,
            out_specs=pl.BlockSpec(memory_space=pl.ANY),
            scratch_shapes=[
                pltpu.VMEM((tiles, 2, TILE, DH), jnp.bfloat16),
                pltpu.VMEM((groups, TILE, DH), jnp.bfloat16),
                pltpu.VMEM((groups, TILE, DH), jnp.bfloat16),
                pltpu.VMEM((SLOTS // 2, TILE, 2 * TILE), jnp.float32),
                pltpu.SMEM((SLOTS, tiles), jnp.int32),
                pltpu.SMEM((heads, tiles), jnp.int32),
                dma((2,)),
                pltpu.SemaphoreType.REGULAR((groups // 2 + 1,)),
                pltpu.SemaphoreType.REGULAR((groups // 2 + 1,)),
                dma,
                dma((2,)),
                dma,
                dma((3,)),
                dma((groups,)),
                dma((groups,)),
                dma((groups,)),
                dma((2, groups)),
                dma((groups,)),
            ],
            compiler_params=pltpu.CompilerParams(
                collective_id=0, has_side_effects=True, vmem_limit_bytes=62 * 2**20
            ),
            cost_estimate=pl.CostEstimate(
                flops=4 * groups * SLOTS * TILE**3,
                bytes_accessed=4 * TILE * groups * DH * 2,
                transcendentals=groups * SLOTS * TILE**2,
            ),
        )(jnp.swapaxes(tile_lists, 1, 2), tile_counts, query_states, key_states, value_states)

    rows = P(("clip", "seq", "help"), None)
    return jax.shard_map(
        shards,
        mesh=mesh,
        in_specs=(rows, rows, rows, P("clip", None, None), P("clip", None)),
        out_specs=rows,
        check_vma=False,
    )
```

```python
import functools
import math

import jax
import jax.numpy as jnp
from jax import lax
from jax.experimental import pallas as pl
from jax.experimental.pallas import tpu as pltpu
from jax.sharding import PartitionSpec as P

MESH = pl.DeviceIdType.MESH
TILE = 128
DH = 128
SLOTS = 16


def spread(n, i):
    half = (i + 1) // 2
    return (half * (2 * (i % 2) - 1) + n) % n


def kernel(
    groups, helpers,
    lists_hbm, counts_hbm, q_hbm, k_hbm, v_hbm, out_ref,
    kv, qs, outs, scores, lists, counts,
    plan_sem, up, down, send_q, send_kv, send_o, send_x,
    recv_q, recv_kv, recv_o, recv_x, recv_far,
):
    z = lax.axis_index("seq")
    x = lax.axis_index("help")
    right = (x + 1) % helpers
    left = (x + helpers - 1) % helpers
    across = (x + 2) % helpers
    above = (z + 1) % groups
    below = (z + groups - 1) % groups
    half = groups // 2
    mine = z * helpers + x

    barrier = pltpu.get_barrier_semaphore()
    for near in (above, below):
        pl.semaphore_signal(barrier, inc=1, device_id={"seq": near}, device_id_type=MESH)
    for near in (left, right):
        pl.semaphore_signal(barrier, inc=1, device_id={"help": near}, device_id_type=MESH)

    plan = [
        pltpu.make_async_copy(lists_hbm.at[z], lists, plan_sem.at[0]),
        pltpu.make_async_copy(counts_hbm, counts, plan_sem.at[1]),
    ]
    for copy in plan:
        copy.start()

    def columns(head):
        return pl.ds(pl.multiple_of(head * DH, DH), DH)

    own = [
        pltpu.make_async_copy(k_hbm.at[:, columns(z)], kv.at[mine, 0], recv_kv.at[z]),
        pltpu.make_async_copy(v_hbm.at[:, columns(z)], kv.at[mine, 1], recv_kv.at[z]),
        pltpu.make_async_copy(q_hbm.at[:, columns(z)], qs.at[z], recv_q.at[z]),
    ]
    for copy in own:
        copy.start()

    def send_keys(there):
        for which, source in ((0, k_hbm), (1, v_hbm)):
            pltpu.make_async_remote_copy(
                src_ref=source.at[:, columns(there)],
                dst_ref=kv.at[mine, which],
                send_sem=send_kv.at[which],
                recv_sem=recv_kv.at[z],
                device_id={"seq": there},
                device_id_type=MESH,
            ).start()

    def tell(distance):
        pl.semaphore_signal(
            up.at[distance + 1], inc=1, device_id={"seq": above}, device_id_type=MESH
        )
        pl.semaphore_signal(
            down.at[distance + 1], inc=1, device_id={"seq": below}, device_id_type=MESH
        )

    pl.semaphore_wait(barrier, 4)
    tell(1)
    send_keys(above)
    send_keys(below)

    def wave(distance, carry):
        pl.semaphore_wait(up.at[distance], 1)
        pl.semaphore_wait(down.at[distance], 1)
        tell(distance)
        send_keys((z + distance) % groups)
        send_keys((z + groups - distance) % groups)
        return carry

    lax.fori_loop(2, half, wave, 0)
    pl.semaphore_wait(up.at[half], 1)
    pl.semaphore_wait(down.at[half], 1)
    send_keys((z + half) % groups)

    def turn(i):
        return (i // 4) * 4 + (z + i) % 4

    def send_queries(i, carry):
        there = turn(i)

        @pl.when(there != z)
        def _():
            pltpu.make_async_remote_copy(
                src_ref=q_hbm.at[:, columns(there)],
                dst_ref=qs.at[z],
                send_sem=send_q,
                recv_sem=recv_q.at[z],
                device_id={"seq": there},
                device_id_type=MESH,
            ).start()

        return carry

    lax.fori_loop(0, groups, send_queries, 0)

    def tile_copy(tile, sem, send, near):
        return pltpu.make_async_remote_copy(
            src_ref=kv.at[tile],
            dst_ref=kv.at[tile],
            send_sem=send_x.at[send],
            recv_sem=sem,
            device_id={"help": near},
            device_id_type=MESH,
        )

    def arrived(ref, sem):
        pltpu.make_async_copy(ref, ref, sem).wait()

    def pass_on(i, carry):
        source = (z + spread(groups, i)) % groups
        tile = source * helpers + x
        arrived(kv.at[tile], recv_kv.at[source])
        tile_copy(tile, recv_x.at[0, source], 0, right).start()
        tile_copy(tile, recv_x.at[1, source], 1, left).start()
        return carry

    def pass_far(i):
        even = (z + spread(groups, i)) % groups
        odd = (z + spread(groups, i + 1)) % groups
        from_left = even * helpers + left
        from_right = odd * helpers + right
        arrived(kv.at[from_left], recv_x.at[0, even])
        tile_copy(from_left, recv_far.at[even], 2, right).start()
        arrived(kv.at[from_right], recv_x.at[1, odd])
        tile_copy(from_right, recv_far.at[odd], 2, left).start()

    def pass_both(i, carry):
        pass_on(2 * i, 0)
        pass_on(2 * i + 1, 0)
        pass_far(2 * i - 2)
        return carry

    pass_on(0, 0)
    pass_on(1, 0)
    lax.fori_loop(1, half, pass_both, 0)
    pass_far(groups - 2)

    def rest(i, carry):
        even = (z + spread(groups, 2 * i)) % groups
        odd = (z + spread(groups, 2 * i + 1)) % groups
        arrived(kv.at[odd * helpers + left], recv_x.at[0, odd])
        arrived(kv.at[even * helpers + right], recv_x.at[1, even])
        arrived(kv.at[even * helpers + across], recv_far.at[even])
        arrived(kv.at[odd * helpers + across], recv_far.at[odd])
        return carry

    lax.fori_loop(0, half, rest, 0)
    for copy in plan:
        copy.wait()

    scale = DH**-0.5 * math.log2(math.e)

    def prepare(source, buffer):
        tile = source * helpers + x
        query = qs[source]
        count = counts[z, tile]
        first = lists[0, tile]
        chosen = [first] + [
            jnp.where(j < count, lists[j, tile], first) for j in range(1, SLOTS)
        ]
        most = None
        for j in range(0, SLOTS, 2):
            keys = jnp.concatenate((kv[chosen[j], 0], kv[chosen[j + 1], 0]), axis=0)
            part = lax.dot_general(
                query, keys, (((1,), (1,)), ((), ())), preferred_element_type=jnp.float32
            )
            scores[buffer, j // 2] = part
            most = part if most is None else jnp.maximum(most, part)
        return jnp.max(most, axis=1, keepdims=True) * scale, count, chosen

    def mix(source, buffer, top, count, chosen):
        total = jnp.zeros((TILE, DH), jnp.float32)
        mixed = jnp.zeros((TILE, DH), jnp.float32)
        for j in range(0, SLOTS, 2):
            weights = []
            for k in (j, j + 1):
                shift = top + jnp.where(k < count, 0.0, 1e30).astype(jnp.float32)
                part = scores[buffer, j // 2, :, (k - j) * TILE : (k - j + 1) * TILE]
                weight = jnp.exp2(part * scale - shift)
                total += weight
                weights.append(weight.astype(jnp.bfloat16))
            values = jnp.concatenate((kv[chosen[j], 1], kv[chosen[j + 1], 1]), axis=0)
            mixed += lax.dot_general(
                jnp.concatenate(weights, axis=1),
                values,
                (((1,), (0,)), ((), ())),
                preferred_element_type=jnp.float32,
            )
        outs[source] = (mixed / jnp.sum(total, axis=1, keepdims=True)).astype(jnp.bfloat16)

    def send_back(source):
        @pl.when(source == z)
        def _():
            pltpu.make_async_copy(outs.at[z], out_ref.at[:, columns(z)], recv_o.at[z]).start()

        @pl.when(source != z)
        def _():
            pltpu.make_async_remote_copy(
                src_ref=outs.at[source],
                dst_ref=out_ref.at[:, columns(z)],
                send_sem=send_o,
                recv_sem=recv_o.at[z],
                device_id={"seq": source},
                device_id_type=MESH,
            ).start()

    def attend(i, carry):
        one, two = turn(2 * i), turn(2 * i + 1)
        arrived(qs.at[one], recv_q.at[one])
        arrived(qs.at[two], recv_q.at[two])
        first, second = prepare(one, 0), prepare(two, 1)
        mix(one, 0, *first)
        mix(two, 1, *second)
        send_back(one)
        send_back(two)
        return carry

    lax.fori_loop(0, half, attend, 0)

    away = groups - 1
    for which in (0, 1):
        arrived(kv.at[pl.ds(0, away), which], send_kv.at[which])
    arrived(qs.at[pl.ds(0, away)], send_q)
    for which in (0, 1, 2):
        arrived(kv.at[pl.ds(0, groups)], send_x.at[which])

    def take(i, carry):
        arrived(out_ref.at[:, columns(i)], recv_o.at[i])
        return carry

    lax.fori_loop(0, groups, take, 0)
    arrived(outs.at[pl.ds(0, away)], send_o)


def solution(mesh):
    groups, helpers = mesh.shape["seq"], mesh.shape["help"]
    tiles = groups * helpers
    dma = pltpu.SemaphoreType.DMA

    def shards(query_states, key_states, value_states, tile_lists, tile_counts):
        heads = tile_lists.shape[0]
        return pl.pallas_call(
            functools.partial(kernel, groups, helpers),
            out_shape=pltpu.VMEM(query_states.shape, jnp.bfloat16),
            in_specs=[pl.BlockSpec(memory_space=pl.ANY)] * 5,
            out_specs=pl.BlockSpec(memory_space=pl.ANY),
            scratch_shapes=[
                pltpu.VMEM((tiles, 2, TILE, DH), jnp.bfloat16),
                pltpu.VMEM((groups, TILE, DH), jnp.bfloat16),
                pltpu.VMEM((groups, TILE, DH), jnp.bfloat16),
                pltpu.VMEM((2, SLOTS // 2, TILE, 2 * TILE), jnp.float32),
                pltpu.SMEM((SLOTS, tiles), jnp.int32),
                pltpu.SMEM((heads, tiles), jnp.int32),
                dma((2,)),
                pltpu.SemaphoreType.REGULAR((groups // 2 + 1,)),
                pltpu.SemaphoreType.REGULAR((groups // 2 + 1,)),
                dma,
                dma((2,)),
                dma,
                dma((3,)),
                dma((groups,)),
                dma((groups,)),
                dma((groups,)),
                dma((2, groups)),
                dma((groups,)),
            ],
            compiler_params=pltpu.CompilerParams(
                collective_id=0, has_side_effects=True, vmem_limit_bytes=62 * 2**20
            ),
            cost_estimate=pl.CostEstimate(
                flops=4 * groups * SLOTS * TILE**3,
                bytes_accessed=4 * TILE * groups * DH * 2,
                transcendentals=groups * SLOTS * TILE**2,
            ),
        )(jnp.swapaxes(tile_lists, 1, 2), tile_counts, query_states, key_states, value_states)

    rows = P(("clip", "seq", "help"), None)
    return jax.shard_map(
        shards,
        mesh=mesh,
        in_specs=(rows, rows, rows, P("clip", None, None), P("clip", None)),
        out_specs=rows,
        check_vma=False,
    )
```
